32 devices in a mesh: groups: 2 (over x), tm: 16 (over z, y, core).
Axes of the slice: x: 2, y: 2, z: 4, core: 2. Of those that a mesh axis runs over, the one named last changes fastest.
Arguments:
- spatial: float32 [256, 256], replicated, as said below
- persistence: float32 [64], P(('groups', 'tm')), parts along dimension 0, as said below
- obs_weight: float32 [64, 256], P(('groups', 'tm')), parts along dimension 0, as said below
- right_side: float32 [64, 256, 256], P(('groups', 'tm')), parts along dimension 0, as said below
Outputs:
- solution: float32 [64, 256, 256], P(('groups', 'tm')), parts along dimension 0
There are 2 independent parts, one for each index of `groups`. The reference program is written for one: setup_inputs(seed, part) draws one part's arguments, and reference() takes and returns one part's arrays. A program takes and returns all parts, laid end to end along the dimension named above; an argument that names none is the same for every part. Nothing has to cross between parts.
Inputs may be any that keep to these rules, and one draw needn't show every extreme that they name: spatial is symmetric and positive definite. `persistence`: every entry lies between 0.9 and 0.997. `obs_weight`: every entry lies between 0.00002 and 0.016. `right_side`: every entry lies between -0.012 and 0.012.
All inputs are finite; a program needn't handle non-finite values.
Results may differ from the reference program's by a relative error of at most 0.0003.
Values sent between devices are 32-bit elements; how exact they have to be, the bound alone decides.
No kernel may reach another device: no remote copies, remote signals or barrier semaphores. Data moves between devices by JAX's collectives and lax.ppermute only.
A program may use at most 128 MiB of HBM per device.

```python
import math
import jax
import jax.numpy as jnp
from jax import lax

NODES = 256
COLUMNS = 256
EPOCH_COUNT = 32


def draw_spatial(key, part):
    key = jax.random.fold_in(key, 11)
    first_key = jax.random.fold_in(key, 0)
    third_key = jax.random.fold_in(key, 2)
    half_range = 0.674 / math.sqrt(NODES)
    entries = jax.random.uniform(first_key, (NODES, NODES), jnp.float32, -half_range, half_range)
    diagonal_values = jax.random.uniform(third_key, (NODES,), jnp.float32, 0.85, 1.25)
    symmetric = 0.5 * (entries + entries.T)
    diagonal_mask = jnp.eye(NODES, dtype=jnp.float32)
    return symmetric * (1.0 - diagonal_mask) + diagonal_mask * diagonal_values[None, :]


def draw_persistence(key, part):
    key = jax.random.fold_in(key, 12)
    first_key, second_random_seed = jax.random.split(key, 2)
    sudden_change_flag = jax.random.randint(second_random_seed, (EPOCH_COUNT,), 0, 256) == 0
    wellposed_sample = jax.random.uniform(first_key, (EPOCH_COUNT,), jnp.float32, 0.99, 0.997)
    return jnp.where(sudden_change_flag, 0.9, wellposed_sample)


def draw_obs_weight(key, part):
    key = jax.random.fold_in(key, 14)
    first_key, second_random_seed, third_key = jax.random.split(key, 3)
    sparse_flag = jax.random.randint(second_random_seed, (EPOCH_COUNT, NODES), 0, 100) == 0
    bulk = jnp.exp(jax.random.uniform(first_key, (EPOCH_COUNT, NODES), jnp.float32, math.log(2e-05), math.log(0.0002)))
    strong_coupling = jnp.exp(jax.random.uniform(third_key, (EPOCH_COUNT, NODES), jnp.float32, math.log(0.004), math.log(0.016)))
    return jnp.where(sparse_flag, strong_coupling, bulk)


def draw_right_side(key, part):
    key = jax.random.fold_in(key, 13)
    return 0.003 * jax.random.truncated_normal(key, -4.0, 4.0, (EPOCH_COUNT, NODES, COLUMNS), jnp.float32)


def setup_inputs(seed: int = 0, part: int = 0) -> dict:
    streams_of = jax.random.split(jax.random.key(seed), 5)
    part_keys = jax.random.split(jax.random.fold_in(streams_of[4], part), 5)
    return {
        "spatial": draw_spatial(jax.random.fold_in(streams_of[4], 71), part),
        "persistence": draw_persistence(jax.random.fold_in(jax.random.fold_in(streams_of[4], part), 71), part),
        "obs_weight": draw_obs_weight(jax.random.fold_in(jax.random.fold_in(streams_of[4], part), 71), part),
        "right_side": draw_right_side(jax.random.fold_in(jax.random.fold_in(streams_of[4], part), 71), part),
    }


HIGH = lax.Precision.HIGHEST

def product(left, right):
    return jnp.matmul(left, right, precision=HIGH)

def forward_solve(factor, values):
    return lax.linalg.triangular_solve(factor, values, left_side=True, lower=True)

def backward_solve(factor, values):
    return lax.linalg.triangular_solve(factor, values, left_side=True, lower=True, transpose_a=True)

def reference(spatial, persistence, obs_weight, right_side):
    node_count = spatial.shape[0]
    identity = jnp.eye(node_count, dtype=spatial.dtype)
    later = jnp.arange(EPOCH_COUNT) > 0
    coupling = jnp.where(later, persistence, jnp.zeros_like(persistence))

    def forward(state, inputs):
        prev_factor, prev_solved = state
        rate, link, weights, source = inputs
        diagonal_block = (1.0 + rate * rate) * spatial + weights[None, :] * identity
        linked = forward_solve(prev_factor, -link * spatial)
        diagonal_block = diagonal_block - product(linked.T, linked)
        reduced = source - product(linked.T, prev_solved)
        factor = jnp.linalg.cholesky(diagonal_block)
        solved = forward_solve(factor, reduced)
        return ((factor, solved), (factor, solved))
    start = (identity, jnp.zeros((node_count, COLUMNS), spatial.dtype))
    unused, stacked = lax.scan(forward, start, (persistence, coupling, obs_weight, right_side))
    factors, solveds = stacked
    following_offdiag_matrix = jnp.concatenate([coupling[1:], jnp.zeros((1,), persistence.dtype)])

    def backward(next_value, inputs):
        factor, solved, link = inputs
        linked = forward_solve(factor, -link * spatial)
        value = backward_solve(factor, solved - product(linked, next_value))
        return (value, value)
    finish = jnp.zeros((node_count, COLUMNS), spatial.dtype)
    unused_last, values = lax.scan(backward, finish, (factors, solveds, following_offdiag_matrix), reverse=True)
    return values
```

```python
import functools

import jax
import jax.numpy as jnp
from jax import lax
from jax.experimental import pallas as pl
from jax.experimental.pallas import tpu as pltpu
from jax.sharding import PartitionSpec as P

F32 = jnp.float32
BF16 = jnp.bfloat16
SUBLANES = 8
ENERGY_TOLERANCE = 1e-12
STEP_LIMIT = 2000
COARSE_LIMIT = 14
FINE_LIMIT = 80


def split(value):
    high = value.astype(BF16)
    return high, (value - high.astype(F32)).astype(BF16)


def dot(left, right):
    return jnp.dot(left, right, preferred_element_type=F32)


def split_dot(left, right_high, right_low):
    high, low = split(left)
    return dot(high, right_high) + dot(low, right_high) + dot(high, right_low)


def exact_dot(left, right):
    return jnp.dot(left, right, preferred_element_type=F32, precision=lax.Precision.HIGHEST)


def loop(count, body, start):
    if count <= 32:
        carry = start
        for i in range(count):
            carry = body(i, carry)
        return carry
    return lax.fori_loop(0, count, body, start)


def eye(size):
    rows = lax.broadcasted_iota(jnp.int32, (size, size), 0)
    columns = lax.broadcasted_iota(jnp.int32, (size, size), 1)
    return jnp.where(rows == columns, 1.0, 0.0).astype(F32)


def row_sum_norm(value):
    return jnp.max(jnp.sum(jnp.abs(value), axis=0, keepdims=True))


def invert(spatial, inverse):
    size = spatial.shape[0]
    identity = eye(size)
    high = spatial.astype(BF16)
    square = dot(high, high)
    bound = jnp.sqrt(row_sum_norm(square)) * 1.02
    scale = 1.9 / bound
    start = scale * (2.0 * identity - scale * spatial)
    inverse[...] = start

    def coarse_step(state):
        count, unused = state
        guess = inverse[...]
        residual = identity - dot(high, guess.astype(BF16))
        inverse[...] = guess + dot(guess.astype(BF16), residual.astype(BF16))
        return count + 1, row_sum_norm(residual)

    def coarse_goes_on(state):
        count, error = state
        return jnp.logical_and(count < COARSE_LIMIT, error > 0.3)

    unused, error = lax.while_loop(coarse_goes_on, coarse_step, (0, F32(1e30)))

    @pl.when(jnp.logical_not(error <= 0.3))
    def restart():
        inverse[...] = start

    def fine_step(state):
        count, unused = state
        guess = inverse[...]
        residual = identity - exact_dot(spatial, guess)
        inverse[...] = guess + exact_dot(guess, residual)
        return count + 1, row_sum_norm(residual)

    def fine_goes_on(state):
        count, error = state
        return jnp.logical_and(count < FINE_LIMIT, error > 0.3)

    lax.while_loop(fine_goes_on, fine_step, (0, F32(1e30)))
    result = inverse[...]
    inverse[...] = 0.5 * (result + result.T)


def solve_kernel(
    segments, per_segment, columns,
    received, spatial, out,
    x, r, p, h, z, q, w, e, d, inverse, s_high, s_low, g_high, g_low,
):
    size = spatial.shape[0]
    steps = segments * per_segment
    block = per_segment * columns

    def at(t):
        if isinstance(t, int):
            return pl.ds(t * columns, columns)
        return pl.ds(pl.multiple_of(t * columns, SUBLANES), columns)

    def source(t):
        if isinstance(t, int):
            return t // per_segment, t % per_segment
        return lax.div(t, per_segment), lax.rem(t, per_segment)

    def right_side(t):
        i, j = source(t)
        if isinstance(t, int):
            return received[i, pl.ds(j * columns, columns), :]
        return received[i, pl.ds(pl.multiple_of(j * columns, SUBLANES), columns), :]

    invert(spatial[...], inverse)
    s_high[...], s_low[...] = split(spatial[...])
    g_high[...], g_low[...] = split(inverse[...])

    def factor(t, last):
        i, j = source(t)
        weight = received[i, pl.ds(block + j, 1), :]
        rate = received[i, pl.ds(block + per_segment + j, 1), :]
        link = rate * last
        inverse_pivot = 1.0 / (1.0 + rate * rate - rate * link)
        w[t] = weight
        e[t] = link
        d[t] = inverse_pivot
        return inverse_pivot

    loop(steps, factor, jnp.zeros((1, size), F32))

    def over_lanes(value):
        return jnp.sum(value, axis=1, keepdims=True)

    def zero():
        return jnp.zeros((columns, size), F32)

    biggest = loop(steps, lambda t, acc: jnp.maximum(acc, jnp.abs(right_side(t))), zero())
    biggest = jnp.max(biggest, axis=1, keepdims=True)
    biggest = jnp.where(biggest > 0.0, biggest, 1.0)
    shrink = 1.0 / biggest

    def load(t, carry):
        r[at(t), :] = right_side(t) * shrink
        x[at(t), :] = zero()
        return carry

    loop(steps, load, 0)

    def precondition():
        z[...] = split_dot(r[...], g_high[...], g_low[...])

    def sweep():
        def down(t, last):
            value = z[at(t), :] + e[t] * last
            z[at(t), :] = value
            return value

        def up(k, carry):
            above, acc = carry
            t = steps - 1 - k
            value = z[at(t), :] * d[t] + above
            z[at(t), :] = value
            return e[t] * value, acc + r[at(t), :] * value

        loop(steps, down, zero())
        unused, acc = loop(steps, up, (zero(), zero()))
        return over_lanes(acc)

    precondition()
    h[...] = z[...]
    energy = sweep()
    p[...] = z[...]
    limit = energy * ENERGY_TOLERANCE

    def goes_on(state):
        count, unused, excess = state
        return jnp.logical_and(count < STEP_LIMIT, excess > 0.0)

    def step(state):
        count, energy, unused = state
        z[...] = split_dot(h[...], s_high[...], s_low[...])

        def curve(t, acc):
            direction = p[at(t), :]
            value = z[at(t), :] + w[t] * direction
            z[at(t), :] = value
            return acc + direction * value

        curvature = over_lanes(loop(steps, curve, zero()))
        alpha = jnp.where(curvature > 0.0, energy / jnp.where(curvature > 0.0, curvature, 1.0), 0.0)

        def advance(t, carry):
            x[at(t), :] += alpha * p[at(t), :]
            r[at(t), :] -= alpha * z[at(t), :]
            return carry

        loop(steps, advance, 0)
        precondition()
        q[...] = z[...]
        new_energy = sweep()
        beta = jnp.where(energy > 0.0, new_energy / jnp.where(energy > 0.0, energy, 1.0), 0.0)

        def turn(t, carry):
            p[at(t), :] = z[at(t), :] + beta * p[at(t), :]
            h[at(t), :] = q[at(t), :] + beta * h[at(t), :]
            return carry

        loop(steps, turn, 0)
        return count + 1, new_energy, jnp.max(new_energy - limit)

    lax.while_loop(goes_on, step, (0, energy, jnp.max(energy)))

    def store(t, carry):
        i, j = source(t)
        if isinstance(t, int):
            rows = pl.ds(j * columns, columns)
        else:
            rows = pl.ds(pl.multiple_of(j * columns, SUBLANES), columns)
        out[i, rows, :] = x[at(t), :] * biggest
        return carry

    loop(steps, store, 0)


def solve(received, spatial, segments, per_segment, columns):
    size = spatial.shape[0]
    steps = segments * per_segment
    rows = steps * columns
    state = pltpu.VMEM((rows, size), F32)
    per_step = pltpu.VMEM((steps, 1, size), F32)
    matrix = pltpu.VMEM((size, size), BF16)
    return pl.pallas_call(
        functools.partial(solve_kernel, segments, per_segment, columns),
        out_shape=jax.ShapeDtypeStruct((segments, per_segment * columns, size), F32),
        in_specs=[pl.BlockSpec(memory_space=pltpu.VMEM)] * 2,
        out_specs=pl.BlockSpec(memory_space=pltpu.VMEM),
        scratch_shapes=[state] * 6 + [per_step] * 3 + [pltpu.VMEM((size, size), F32)] + [matrix] * 4,
        compiler_params=pltpu.CompilerParams(vmem_limit_bytes=40 * 2**20),
        name="solve",
    )(received, spatial)


def body(spatial, persistence, obs_weight, right_side):
    devices = lax.axis_size("tm")
    per_segment, size, column_count = right_side.shape
    columns = column_count // devices
    padded = -(-columns // SUBLANES) * SUBLANES

    parts = jnp.swapaxes(right_side, 1, 2).reshape(per_segment, devices, columns, size)
    parts = jnp.swapaxes(parts, 0, 1).reshape(devices, per_segment * columns, size)
    rates = jnp.broadcast_to(persistence[:, None], (per_segment, size))
    shared = jnp.concatenate([obs_weight, rates])
    fill = -(per_segment * columns + 2 * per_segment) % SUBLANES
    shared = jnp.pad(shared, ((0, fill), (0, 0)))
    shared = jnp.broadcast_to(shared[None], (devices,) + shared.shape)
    received = lax.all_to_all(jnp.concatenate([parts, shared], axis=1), "tm", 0, 0, tiled=True)
    if padded != columns:
        block = received[:, : per_segment * columns].reshape(devices, per_segment, columns, size)
        block = jnp.pad(block, ((0, 0), (0, 0), (0, padded - columns), (0, 0)))
        block = block.reshape(devices, per_segment * padded, size)
        received = jnp.concatenate([block, received[:, per_segment * columns :]], axis=1)
    solved = solve(received, spatial, devices, per_segment, padded)
    if padded != columns:
        solved = solved.reshape(devices, per_segment, padded, size)[:, :, :columns]
        solved = solved.reshape(devices, per_segment * columns, size)
    returned = lax.all_to_all(solved, "tm", 0, 0, tiled=True)
    returned = returned.reshape(devices, per_segment, columns, size)
    return jnp.transpose(returned, (1, 3, 0, 2)).reshape(per_segment, size, column_count)


def solution(mesh):
    placed = (P(), P(("groups", "tm")), P(("groups", "tm"), None), P(("groups", "tm"), None, None))
    return jax.shard_map(
        body, mesh=mesh, in_specs=placed, out_specs=P(("groups", "tm"), None, None), check_vma=False
    )
```

```python
import functools

import jax
import jax.numpy as jnp
from jax import lax
from jax.experimental import pallas as pl
from jax.experimental.pallas import tpu as pltpu
from jax.sharding import PartitionSpec as P

F32 = jnp.float32
BF16 = jnp.bfloat16
SUBLANES = 8
ENERGY_TOLERANCE = 1e-12
STEP_LIMIT = 2000
COARSE_LIMIT = 14
FINE_LIMIT = 80


def split(value):
    high = value.astype(BF16)
    return high, (value - high.astype(F32)).astype(BF16)


def dot(left, right):
    return jnp.dot(left, right, preferred_element_type=F32)


def split_dot(left, right_high, right_low):
    high, low = split(left)
    return dot(high, right_high) + dot(low, right_high) + dot(high, right_low)


def exact_dot(left, right):
    return jnp.dot(left, right, preferred_element_type=F32, precision=lax.Precision.HIGHEST)


def loop(count, body, start):
    if count <= 32:
        carry = start
        for i in range(count):
            carry = body(i, carry)
        return carry
    return lax.fori_loop(0, count, body, start)


def eye(size):
    rows = lax.broadcasted_iota(jnp.int32, (size, size), 0)
    columns = lax.broadcasted_iota(jnp.int32, (size, size), 1)
    return jnp.where(rows == columns, 1.0, 0.0).astype(F32)


def row_sum_norm(value):
    return jnp.max(jnp.sum(jnp.abs(value), axis=0, keepdims=True))


def invert(spatial, inverse):
    size = spatial.shape[0]
    identity = eye(size)
    high = spatial.astype(BF16)
    square = dot(high, high)
    bound = jnp.sqrt(row_sum_norm(square)) * 1.02
    scale = 1.9 / bound
    start = scale * (2.0 * identity - scale * spatial)
    inverse[...] = start

    def coarse_step(state):
        count, unused = state
        guess = inverse[...]
        residual = identity - dot(high, guess.astype(BF16))
        inverse[...] = guess + dot(guess.astype(BF16), residual.astype(BF16))
        return count + 1, row_sum_norm(residual)

    def coarse_goes_on(state):
        count, error = state
        return jnp.logical_and(count < COARSE_LIMIT, error > 0.3)

    unused, error = lax.while_loop(coarse_goes_on, coarse_step, (0, F32(1e30)))

    @pl.when(jnp.logical_not(error <= 0.3))
    def restart():
        inverse[...] = start

    def fine_step(state):
        count, unused = state
        guess = inverse[...]
        residual = identity - exact_dot(spatial, guess)
        inverse[...] = guess + exact_dot(guess, residual)
        return count + 1, row_sum_norm(residual)

    def fine_goes_on(state):
        count, error = state
        return jnp.logical_and(count < FINE_LIMIT, error > 0.3)

    lax.while_loop(fine_goes_on, fine_step, (0, F32(1e30)))
    result = inverse[...]
    inverse[...] = 0.5 * (result + result.T)


def invert_kernel(spatial, s_high, s_low, g_high, g_low, inverse):
    s_high[...], s_low[...] = split(spatial[...])
    invert(spatial[...], inverse)
    g_high[...], g_low[...] = split(inverse[...])


def halves_with_inverse(spatial):
    size = spatial.shape[0]
    return pl.pallas_call(
        invert_kernel,
        out_shape=[jax.ShapeDtypeStruct((size, size), BF16)] * 4,
        in_specs=[pl.BlockSpec(memory_space=pltpu.VMEM)],
        out_specs=[pl.BlockSpec(memory_space=pltpu.VMEM)] * 4,
        scratch_shapes=[pltpu.VMEM((size, size), F32)],
        cost_estimate=pl.CostEstimate(flops=48 * size**3, bytes_accessed=16 * size**2, transcendentals=0),
        compiler_params=pltpu.CompilerParams(vmem_limit_bytes=16 * 2**20),
        name="invert",
    )(spatial)


def solve_kernel(
    segments, per_segment, columns,
    received, s_high, s_low, g_high, g_low, out,
    x, r, p, h, z, q, w, e, d,
):
    size = s_high.shape[0]
    steps = segments * per_segment
    block = per_segment * columns

    def at(t):
        if isinstance(t, int):
            return pl.ds(t * columns, columns)
        return pl.ds(pl.multiple_of(t * columns, SUBLANES), columns)

    def source(t):
        if isinstance(t, int):
            return t // per_segment, t % per_segment
        return lax.div(t, per_segment), lax.rem(t, per_segment)

    def right_side(t):
        i, j = source(t)
        if isinstance(t, int):
            return received[i, pl.ds(j * columns, columns), :]
        return received[i, pl.ds(pl.multiple_of(j * columns, SUBLANES), columns), :]

    def factor(t, last):
        i, j = source(t)
        weight = received[i, pl.ds(block + j, 1), :]
        rate = received[i, pl.ds(block + per_segment + j, 1), :]
        link = rate * last
        inverse_pivot = 1.0 / (1.0 + rate * rate - rate * link)
        w[t] = weight
        e[t] = link
        d[t] = inverse_pivot
        return inverse_pivot

    loop(steps, factor, jnp.zeros((1, size), F32))

    def over_lanes(value):
        return jnp.sum(value, axis=1, keepdims=True)

    def zero():
        return jnp.zeros((columns, size), F32)

    biggest = loop(steps, lambda t, acc: jnp.maximum(acc, jnp.abs(right_side(t))), zero())
    biggest = jnp.max(biggest, axis=1, keepdims=True)
    biggest = jnp.where(biggest > 0.0, biggest, 1.0)
    shrink = 1.0 / biggest

    def load(t, carry):
        r[at(t), :] = right_side(t) * shrink
        x[at(t), :] = zero()
        return carry

    loop(steps, load, 0)

    def precondition():
        z[...] = split_dot(r[...], g_high[...], g_low[...])

    def sweep():
        def down(t, last):
            value = z[at(t), :] + e[t] * last
            z[at(t), :] = value
            return value

        def up(k, carry):
            above, acc = carry
            t = steps - 1 - k
            value = z[at(t), :] * d[t] + above
            z[at(t), :] = value
            return e[t] * value, acc + r[at(t), :] * value

        loop(steps, down, zero())
        unused, acc = loop(steps, up, (zero(), zero()))
        return over_lanes(acc)

    precondition()
    h[...] = z[...]
    energy = sweep()
    p[...] = z[...]
    limit = energy * ENERGY_TOLERANCE

    def goes_on(state):
        count, unused, excess = state
        return jnp.logical_and(count < STEP_LIMIT, excess > 0.0)

    def step(state):
        count, energy, unused = state
        z[...] = split_dot(h[...], s_high[...], s_low[...])

        def curve(t, acc):
            direction = p[at(t), :]
            value = z[at(t), :] + w[t] * direction
            z[at(t), :] = value
            return acc + direction * value

        curvature = over_lanes(loop(steps, curve, zero()))
        alpha = jnp.where(curvature > 0.0, energy / jnp.where(curvature > 0.0, curvature, 1.0), 0.0)

        def advance(t, carry):
            x[at(t), :] += alpha * p[at(t), :]
            r[at(t), :] -= alpha * z[at(t), :]
            return carry

        loop(steps, advance, 0)
        precondition()
        q[...] = z[...]
        new_energy = sweep()
        beta = jnp.where(energy > 0.0, new_energy / jnp.where(energy > 0.0, energy, 1.0), 0.0)

        def turn(t, carry):
            p[at(t), :] = z[at(t), :] + beta * p[at(t), :]
            h[at(t), :] = q[at(t), :] + beta * h[at(t), :]
            return carry

        loop(steps, turn, 0)
        return count + 1, new_energy, jnp.max(new_energy - limit)

    lax.while_loop(goes_on, step, (0, energy, jnp.max(energy)))

    def store(t, carry):
        i, j = source(t)
        if isinstance(t, int):
            rows = pl.ds(j * columns, columns)
        else:
            rows = pl.ds(pl.multiple_of(j * columns, SUBLANES), columns)
        out[i, rows, :] = x[at(t), :] * biggest
        return carry

    loop(steps, store, 0)


def solve(received, matrices, segments, per_segment, columns):
    size = received.shape[2]
    steps = segments * per_segment
    rows = steps * columns
    state = pltpu.VMEM((rows, size), F32)
    per_step = pltpu.VMEM((steps, 1, size), F32)
    return pl.pallas_call(
        functools.partial(solve_kernel, segments, per_segment, columns),
        out_shape=jax.ShapeDtypeStruct((segments, per_segment * columns, size), F32),
        in_specs=[pl.BlockSpec(memory_space=pltpu.VMEM)] * 5,
        out_specs=pl.BlockSpec(memory_space=pltpu.VMEM),
        scratch_shapes=[state] * 6 + [per_step] * 3,
        compiler_params=pltpu.CompilerParams(vmem_limit_bytes=40 * 2**20),
        name="solve",
    )(received, *matrices)


def body(spatial, persistence, obs_weight, right_side):
    devices = lax.axis_size("tm")
    per_segment, size, column_count = right_side.shape
    columns = column_count // devices
    padded = -(-columns // SUBLANES) * SUBLANES

    parts = jnp.swapaxes(right_side, 1, 2).reshape(per_segment, devices, columns, size)
    parts = jnp.swapaxes(parts, 0, 1).reshape(devices, per_segment * columns, size)
    rates = jnp.broadcast_to(persistence[:, None], (per_segment, size))
    shared = jnp.concatenate([obs_weight, rates])
    fill = -(per_segment * columns + 2 * per_segment) % SUBLANES
    shared = jnp.pad(shared, ((0, fill), (0, 0)))
    shared = jnp.broadcast_to(shared[None], (devices,) + shared.shape)
    received = lax.all_to_all(jnp.concatenate([parts, shared], axis=1), "tm", 0, 0, tiled=True)
    if padded != columns:
        block = received[:, : per_segment * columns].reshape(devices, per_segment, columns, size)
        block = jnp.pad(block, ((0, 0), (0, 0), (0, padded - columns), (0, 0)))
        block = block.reshape(devices, per_segment * padded, size)
        received = jnp.concatenate([block, received[:, per_segment * columns :]], axis=1)
    solved = solve(received, halves_with_inverse(spatial), devices, per_segment, padded)
    if padded != columns:
        solved = solved.reshape(devices, per_segment, padded, size)[:, :, :columns]
        solved = solved.reshape(devices, per_segment * columns, size)
    returned = lax.all_to_all(solved, "tm", 0, 0, tiled=True)
    returned = returned.reshape(devices, per_segment, columns, size)
    return jnp.transpose(returned, (1, 3, 0, 2)).reshape(per_segment, size, column_count)


def solution(mesh):
    placed = (P(), P(("groups", "tm")), P(("groups", "tm"), None), P(("groups", "tm"), None, None))
    return jax.shard_map(
        body, mesh=mesh, in_specs=placed, out_specs=P(("groups", "tm"), None, None), check_vma=False
    )
```

```python
import functools

import jax
import jax.numpy as jnp
from jax import lax
from jax.experimental import pallas as pl
from jax.experimental.pallas import tpu as pltpu
from jax.sharding import PartitionSpec as P

F32 = jnp.float32
BF16 = jnp.bfloat16
SUBLANES = 8
LANES = 128
TOLERANCE = 1e-5
STEP_LIMIT = 2000
COARSE_LIMIT = 14
FINE_LIMIT = 80
INVERSE_TOLERANCE = 1e-5
CORRECTION_TOLERANCE = 1e-6
REFINEMENT_LIMIT = 8


def split(value):
    high = value.astype(BF16)
    return high, (value - high.astype(F32)).astype(BF16)


def dot(left, right):
    return jnp.dot(left, right, preferred_element_type=F32)


def split_dot(left, right_high, right_low):
    high, low = split(left)
    return dot(high, right_high) + dot(low, right_high) + dot(high, right_low)


def exact_dot(left, right):
    return jnp.dot(left, right, preferred_element_type=F32, precision=lax.Precision.HIGHEST)


def loop(count, body, start):
    if count <= 32:
        carry = start
        for i in range(count):
            carry = body(i, carry)
        return carry
    return lax.fori_loop(0, count, body, start)


def eye(size):
    rows = lax.broadcasted_iota(jnp.int32, (size, size), 0)
    columns = lax.broadcasted_iota(jnp.int32, (size, size), 1)
    return jnp.where(rows == columns, 1.0, 0.0).astype(F32)


def row_sum_norm(value):
    return jnp.max(jnp.sum(jnp.abs(value), axis=0, keepdims=True))


def invert(spatial, inverse):
    size = spatial.shape[0]
    identity = eye(size)
    high = spatial.astype(BF16)
    square = dot(high, high)
    bound = jnp.sqrt(row_sum_norm(square)) * 1.02
    scale = 1.9 / bound
    start = scale * (2.0 * identity - scale * spatial)
    inverse[...] = start

    def coarse_step(state):
        count, unused = state
        guess = inverse[...]
        residual = identity - dot(high, guess.astype(BF16))
        inverse[...] = guess + dot(guess.astype(BF16), residual.astype(BF16))
        return count + 1, row_sum_norm(residual)

    def coarse_goes_on(state):
        count, error = state
        return jnp.logical_and(count < COARSE_LIMIT, error > 0.3)

    unused, error = lax.while_loop(coarse_goes_on, coarse_step, (0, F32(1e30)))

    @pl.when(jnp.logical_not(error <= 0.3))
    def restart():
        inverse[...] = start

    def fine_step(state):
        count, unused = state
        guess = inverse[...]
        residual = identity - exact_dot(spatial, guess)
        inverse[...] = guess + exact_dot(guess, residual)
        return count + 1, row_sum_norm(residual)

    def fine_goes_on(state):
        count, error = state
        return jnp.logical_and(count < FINE_LIMIT, error > 1e-3)

    lax.while_loop(fine_goes_on, fine_step, (0, F32(1e30)))
    result = inverse[...]
    result = 0.5 * (result + result.T)
    inverse[...] = result
    residual = identity - exact_dot(spatial, result)
    return jnp.sum(residual * residual) / size


def invert_kernel(spatial, inverse, high, low, error):
    error[0, 0] = invert(spatial[...], inverse)
    high[...], low[...] = split(inverse[...])


def invert_spatial(spatial):
    size = spatial.shape[0]
    half = jax.ShapeDtypeStruct((size, size), BF16)
    full = jax.ShapeDtypeStruct((size, size), F32)
    vmem, smem = pl.BlockSpec(memory_space=pltpu.VMEM), pl.BlockSpec(memory_space=pltpu.SMEM)
    return pl.pallas_call(
        invert_kernel,
        out_shape=[full, half, half, jax.ShapeDtypeStruct((1, 1), F32)],
        in_specs=[vmem],
        out_specs=[vmem, vmem, vmem, smem],
        cost_estimate=pl.CostEstimate(flops=80 * size**3, bytes_accessed=16 * size**2, transcendentals=0),
        compiler_params=pltpu.CompilerParams(vmem_limit_bytes=16 * 2**20),
        name="invert",
    )(spatial)


def pack_kernel(rates, right_side, weights, out):
    steps, size, column_count = right_side.shape
    devices = out.shape[0]
    columns = column_count // devices
    halves = size // LANES
    tail = steps * halves * columns
    for e in range(steps):
        turned = right_side[e].T
        for i in range(devices):
            for k in range(halves):
                out[i, pl.ds((e * halves + k) * columns, columns), :] = turned[
                    i * columns : (i + 1) * columns, k * LANES : (k + 1) * LANES
                ]
    row = lax.broadcasted_iota(jnp.int32, (out.shape[1] - tail, LANES), 0)
    last = jnp.zeros(row.shape, F32)
    for e in range(steps):
        for k in range(halves):
            weight = weights[pl.ds(e, 1), pl.ds(k * LANES, LANES)]
            last = jnp.where(row == e * halves + k, weight, last)
        last = jnp.where(row == steps * halves + e, rates[e], last)
    for i in range(devices):
        out[i, pl.ds(tail, row.shape[0]), :] = last


def pack(persistence, right_side, weights, devices):
    steps, size, column_count = right_side.shape
    halves = size // LANES
    rows = steps * halves * (column_count // devices)
    total = rows + steps * halves + steps
    total += -total % SUBLANES
    vmem, smem = pl.BlockSpec(memory_space=pltpu.VMEM), pl.BlockSpec(memory_space=pltpu.SMEM)
    return pl.pallas_call(
        pack_kernel,
        out_shape=jax.ShapeDtypeStruct((devices, total, LANES), F32),
        in_specs=[smem, vmem, vmem],
        out_specs=vmem,
        compiler_params=pltpu.CompilerParams(vmem_limit_bytes=16 * 2**20),
        name="pack",
    )(persistence, right_side, weights)


def solve_kernel(
    segments, per_segment, columns,
    received, error, spatial, g, g_high, g_low, out,
    x, r, p, z, w, e, d, rates,
):
    size = g.shape[0]
    steps = segments * per_segment
    halves = size // LANES
    tail = per_segment * halves * columns

    def rows(start):
        if isinstance(start, int):
            return pl.ds(start, columns)
        return pl.ds(pl.multiple_of(start, SUBLANES), columns)

    def at(t):
        return rows(t * columns)

    def source(t):
        if isinstance(t, int):
            return t // per_segment, t % per_segment
        return lax.div(t, per_segment), lax.rem(t, per_segment)

    def lanes(pieces):
        return jnp.concatenate(pieces, axis=1)

    def right_side(t):
        i, j = source(t)
        return lanes([received[i, rows((j * halves + k) * columns), :] for k in range(halves)])

    def over_lanes(value):
        return jnp.sum(value, axis=1, keepdims=True)

    def zero():
        return jnp.zeros((columns, size), F32)

    def ratio(top, bottom):
        return jnp.where(bottom > 0.0, top / jnp.where(bottom > 0.0, bottom, 1.0), 0.0)

    def factor(t, last):
        i, j = source(t)
        w[t] = lanes([received[i, pl.ds(tail + j * halves + k, 1), :] for k in range(halves)])
        rate = received[i, pl.ds(tail + per_segment * halves + j, 1), :]
        link = rate * last
        inverse_pivot = 1.0 / (1.0 + rate * rate - rate * link)
        rates[t] = lanes([rate] * halves)
        e[t] = lanes([link] * halves)
        d[t] = lanes([inverse_pivot] * halves)
        return inverse_pivot

    loop(steps, factor, jnp.zeros((1, LANES), F32))

    biggest = loop(steps, lambda t, acc: jnp.maximum(acc, jnp.abs(right_side(t))), zero())
    biggest = jnp.max(biggest, axis=1, keepdims=True)
    biggest = jnp.where(biggest > 0.0, biggest, 1.0)
    shrink = 1.0 / biggest

    def load(t, carry):
        r[at(t), :] = right_side(t) * shrink
        return carry

    loop(steps, load, 0)

    def down(t, last):
        value = z[at(t), :] + e[t] * last
        z[at(t), :] = value
        return value

    def start(first):
        z[...] = exact_dot(r[...], g[...])
        loop(steps, down, zero())

        def up(k, carry):
            above, acc = carry
            t = steps - 1 - k
            value = z[at(t), :] * d[t] + above
            x[at(t), :] = value if first else x[at(t), :] + value
            r[at(t), :] = value
            p[at(t), :] = value
            return e[t] * value, acc + w[t] * value * value

        unused, acc = loop(steps, up, (zero(), zero()))
        return over_lanes(acc)

    def weigh(t, carry):
        z[at(t), :] = w[t] * p[at(t), :]
        return carry

    def step(state):
        count, square, limit, unused = state
        loop(steps, weigh, 0)
        z[...] = split_dot(z[...], g_high[...], g_low[...])
        loop(steps, down, zero())

        def up(k, carry):
            above, own, cross = carry
            t = steps - 1 - k
            value = z[at(t), :] * d[t] + above
            z[at(t), :] = value
            direction = p[at(t), :]
            weighted = w[t] * direction
            return e[t] * value, own + weighted * direction, cross + weighted * value

        unused, own, cross = loop(steps, up, (zero(), zero(), zero()))
        own, cross = over_lanes(own), over_lanes(cross)
        alpha = ratio(square, own + cross)

        def advance(t, acc):
            change = z[at(t), :]
            x[at(t), :] -= alpha * change
            value = r[at(t), :] - alpha * (p[at(t), :] + change)
            r[at(t), :] = value
            return acc + w[t] * value * value

        new_square = over_lanes(loop(steps, advance, zero()))
        beta = ratio(new_square, square)

        def turn(t, carry):
            p[at(t), :] = r[at(t), :] + beta * p[at(t), :]
            return carry

        loop(steps, turn, 0)
        share = ratio(cross, own + cross)
        return count + 1, new_square, limit, jnp.max(share * share * new_square - limit)

    def goes_on(state):
        count, unused, unused_limit, excess = state
        return jnp.logical_and(count < STEP_LIMIT, excess > 0.0)

    def iterate(square):
        lax.while_loop(goes_on, step, (0, square, square * TOLERANCE**2, jnp.max(square)))

    whole_square = start(True)
    iterate(whole_square)

    def refine(state):
        count, unused = state

        def combine(t, last):
            here = x[at(t), :]
            after = jnp.minimum(t + 1, steps - 1)
            link = jnp.where(t + 1 < steps, 1.0, 0.0) * rates[after]
            value = (1.0 + rates[t] * rates[t]) * here - rates[t] * last - link * x[at(after), :]
            z[at(t), :] = value
            return here

        lax.fori_loop(0, steps, combine, zero())
        z[...] = exact_dot(z[...], spatial[...])

        def subtract(t, carry):
            i, j = source(t)
            r[at(t), :] = right_side(t) * shrink - z[at(t), :] - w[t] * x[at(t), :]
            return carry

        lax.fori_loop(0, steps, subtract, 0)
        square = start(False)
        iterate(square)
        return count + 1, jnp.max(square - whole_square * CORRECTION_TOLERANCE**2)

    def refines(state):
        count, excess = state
        return jnp.logical_and(count < REFINEMENT_LIMIT, excess > 0.0)

    lax.while_loop(refines, refine, (0, error[0, 0] - INVERSE_TOLERANCE**2))

    def store(t, carry):
        i, j = source(t)
        out[i, rows(j * columns), :] = x[at(t), :] * biggest
        return carry

    loop(steps, store, 0)


def solve(received, spatial, inverse, segments, per_segment, columns):
    size = spatial.shape[0]
    steps = segments * per_segment
    state = pltpu.VMEM((steps * columns, size), F32)
    per_step = pltpu.VMEM((steps, 1, size), F32)
    full, high, low, error = inverse
    vmem, smem = pl.BlockSpec(memory_space=pltpu.VMEM), pl.BlockSpec(memory_space=pltpu.SMEM)
    return pl.pallas_call(
        functools.partial(solve_kernel, segments, per_segment, columns),
        out_shape=jax.ShapeDtypeStruct((segments, per_segment * columns, size), F32),
        in_specs=[vmem, smem, vmem, vmem, vmem, vmem],
        out_specs=vmem,
        scratch_shapes=[state] * 4 + [per_step] * 4,
        compiler_params=pltpu.CompilerParams(vmem_limit_bytes=40 * 2**20),
        name="solve",
    )(received, error, spatial, full, high, low)


def pad_columns(received, per_segment, halves, columns, padded):
    devices, total, width = received.shape
    rows = per_segment * halves * columns
    block = received[:, :rows].reshape(devices, per_segment * halves, columns, width)
    block = jnp.pad(block, ((0, 0), (0, 0), (0, padded - columns), (0, 0)))
    return jnp.concatenate([block.reshape(devices, -1, width), received[:, rows:]], axis=1)


def body(spatial, persistence, obs_weight, right_side):
    devices = lax.axis_size("tm")
    per_segment, size, column_count = right_side.shape
    columns = column_count // devices
    padded = -(-columns // SUBLANES) * SUBLANES
    inverse = invert_spatial(spatial)
    packed = pack(persistence, right_side, obs_weight, devices)
    received = lax.all_to_all(packed, "tm", 0, 0, tiled=True)
    if padded != columns:
        received = pad_columns(received, per_segment, size // LANES, columns, padded)
    solved = solve(received, spatial, inverse, devices, per_segment, padded)
    if padded != columns:
        solved = solved.reshape(devices, per_segment, padded, size)[:, :, :columns]
        solved = solved.reshape(devices, per_segment * columns, size)
    returned = lax.all_to_all(solved, "tm", 0, 0, tiled=True)
    returned = returned.reshape(devices, per_segment, columns, size)
    return jnp.transpose(returned, (1, 3, 0, 2)).reshape(per_segment, size, column_count)


def solution(mesh):
    placed = (P(), P(("groups", "tm")), P(("groups", "tm"), None), P(("groups", "tm"), None, None))
    return jax.shard_map(
        body, mesh=mesh, in_specs=placed, out_specs=P(("groups", "tm"), None, None), check_vma=False
    )
```

```python
import functools

import jax
import jax.numpy as jnp
from jax import lax
from jax.experimental import pallas as pl
from jax.experimental.pallas import tpu as pltpu
from jax.sharding import PartitionSpec as P

F32 = jnp.float32
BF16 = jnp.bfloat16
SUBLANES = 8
LANES = 128
CHUNKS = 1
TOLERANCE = 1e-5
STEP_LIMIT = 2000
COARSE_LIMIT = 14
FINE_LIMIT = 80
INVERSE_TOLERANCE = 1e-5
EASY_STEPS = 6
CORRECTION_TOLERANCE = 1e-6
REFINEMENT_LIMIT = 8


def split(value):
    high = value.astype(BF16)
    return high, (value - high.astype(F32)).astype(BF16)


def dot(left, right):
    return jnp.dot(left, right, preferred_element_type=F32)


def split_dot(left, right_high, right_low):
    high, low = split(left)
    return dot(high, right_high) + dot(low, right_high) + dot(high, right_low)


def exact_dot(left, right):
    return jnp.dot(left, right, preferred_element_type=F32, precision=lax.Precision.HIGHEST)


def loop(count, body, start):
    if count <= 32:
        carry = start
        for i in range(count):
            carry = body(i, carry)
        return carry
    return lax.fori_loop(0, count, body, start)


def eye(size):
    rows = lax.broadcasted_iota(jnp.int32, (size, size), 0)
    columns = lax.broadcasted_iota(jnp.int32, (size, size), 1)
    return jnp.where(rows == columns, 1.0, 0.0).astype(F32)


def row_sum_norm(value):
    return jnp.max(jnp.sum(jnp.abs(value), axis=0, keepdims=True))


def invert(spatial, inverse):
    size = spatial.shape[0]
    identity = eye(size)
    high = spatial.astype(BF16)
    square = dot(high, high)
    bound = jnp.sqrt(row_sum_norm(square)) * 1.02
    scale = 1.9 / bound
    start = scale * (2.0 * identity - scale * spatial)
    inverse[...] = start

    def coarse_step(state):
        count, unused = state
        guess = inverse[...]
        residual = identity - dot(high, guess.astype(BF16))
        inverse[...] = guess + dot(guess.astype(BF16), residual.astype(BF16))
        return count + 1, row_sum_norm(residual)

    def coarse_goes_on(state):
        count, error = state
        return jnp.logical_and(count < COARSE_LIMIT, error > 0.3)

    unused, error = lax.while_loop(coarse_goes_on, coarse_step, (0, F32(1e30)))

    @pl.when(jnp.logical_not(error <= 0.3))
    def restart():
        inverse[...] = start

    def fine_step(state):
        count, unused = state
        guess = inverse[...]
        residual = identity - exact_dot(spatial, guess)
        inverse[...] = guess + exact_dot(guess, residual)
        return count + 1, row_sum_norm(residual)

    def fine_goes_on(state):
        count, error = state
        return jnp.logical_and(count < FINE_LIMIT, error > 1e-3)

    lax.while_loop(fine_goes_on, fine_step, (0, F32(1e30)))
    result = inverse[...]
    result = 0.5 * (result + result.T)
    inverse[...] = result
    residual = identity - exact_dot(spatial, result)
    return jnp.sum(residual * residual) / size


def invert_kernel(spatial, inverse, high, low, error):
    error[0, 0] = invert(spatial[...], inverse)
    high[...], low[...] = split(inverse[...])


def invert_spatial(spatial):
    size = spatial.shape[0]
    half = jax.ShapeDtypeStruct((size, size), BF16)
    full = jax.ShapeDtypeStruct((size, size), F32)
    vmem, smem = pl.BlockSpec(memory_space=pltpu.VMEM), pl.BlockSpec(memory_space=pltpu.SMEM)
    return pl.pallas_call(
        invert_kernel,
        out_shape=[full, half, half, jax.ShapeDtypeStruct((1, 1), F32)],
        in_specs=[vmem],
        out_specs=[vmem, vmem, vmem, smem],
        cost_estimate=pl.CostEstimate(flops=80 * size**3, bytes_accessed=16 * size**2, transcendentals=0),
        compiler_params=pltpu.CompilerParams(vmem_limit_bytes=16 * 2**20),
        name="invert",
    )(spatial)


def tail_rows(per_segment, halves):
    rows = per_segment * halves + per_segment
    return rows + -rows % SUBLANES


def pack_kernel(chunks, rates, right_side, weights, *refs):
    outs, (turned, source, rate, weight, arrivals, departures) = refs[:chunks], refs[chunks:]
    steps, size, column_count = right_side.shape
    devices = outs[0].shape[0]
    columns = column_count // devices
    part = columns // chunks
    halves = size // LANES
    block = steps * halves * part
    tail = tail_rows(steps, halves)
    loads = [pltpu.make_async_copy(right_side.at[e], source.at[e], arrivals.at[e]) for e in range(steps)]
    loads.append(pltpu.make_async_copy(rates, rate, arrivals.at[steps]))
    loads.append(pltpu.make_async_copy(weights, weight, arrivals.at[steps + 1]))
    for copy in loads:
        copy.start()
    for copy in loads[steps:]:
        copy.wait()
    row = lax.broadcasted_iota(jnp.int32, (tail, LANES), 0)
    last = jnp.zeros(row.shape, F32)
    for e in range(steps):
        for k in range(halves):
            last = jnp.where(row == e * halves + k, weight[pl.ds(e, 1), pl.ds(k * LANES, LANES)], last)
        last = jnp.where(row == steps * halves + e, rate[e], last)
    for i in range(devices):
        turned[0, i, pl.ds(block, tail), :] = last
    for e in range(steps):
        loads[e].wait()
        value = source[e].T
        for i in range(devices):
            for c in range(chunks):
                for k in range(halves):
                    first = i * columns + c * part
                    turned[c, i, pl.ds((e * halves + k) * part, part), :] = value[
                        first : first + part, k * LANES : (k + 1) * LANES
                    ]
    stores = [
        pltpu.make_async_copy(turned.at[c, :, pl.ds(0, out.shape[1]), :], out, departures.at[c])
        for c, out in enumerate(outs)
    ]
    for copy in stores:
        copy.start()
    for copy in stores:
        copy.wait()


def pack(persistence, right_side, weights, devices, chunks):
    steps, size, column_count = right_side.shape
    halves = size // LANES
    rows = steps * halves * (column_count // devices // chunks)
    total = rows + tail_rows(steps, halves)
    anywhere = pl.BlockSpec(memory_space=pl.ANY)
    shapes = [total] + [rows] * (chunks - 1)
    return pl.pallas_call(
        functools.partial(pack_kernel, chunks),
        out_shape=[jax.ShapeDtypeStruct((devices, n, LANES), F32) for n in shapes],
        in_specs=[anywhere] * 3,
        out_specs=[anywhere] * chunks,
        scratch_shapes=[
            pltpu.VMEM((chunks, devices, total, LANES), F32),
            pltpu.VMEM(right_side.shape, F32),
            pltpu.SMEM(persistence.shape, F32),
            pltpu.VMEM(weights.shape, F32),
            pltpu.SemaphoreType.DMA((steps + 2,)),
            pltpu.SemaphoreType.DMA((chunks,)),
        ],
        compiler_params=pltpu.CompilerParams(vmem_limit_bytes=56 * 2**20),
        name="pack",
    )(persistence, right_side, weights)


def solve_kernel(
    segments, per_segment, columns,
    received, shared, error, spatial, g, g_high, g_low, out,
    x, r, p, z, w, e, d, rates,
):
    size = g.shape[0]
    steps = segments * per_segment
    halves = size // LANES
    tail = shared.shape[1] - tail_rows(per_segment, halves)

    def rows(start):
        if isinstance(start, int):
            return pl.ds(start, columns)
        return pl.ds(pl.multiple_of(start, SUBLANES), columns)

    def at(t):
        return rows(t * columns)

    def source(t):
        if isinstance(t, int):
            return t // per_segment, t % per_segment
        return lax.div(t, per_segment), lax.rem(t, per_segment)

    def lanes(pieces):
        return jnp.concatenate(pieces, axis=1)

    def right_side(t):
        i, j = source(t)
        return lanes([received[i, rows((j * halves + k) * columns), :] for k in range(halves)])

    def over_lanes(value):
        return jnp.sum(value, axis=1, keepdims=True)

    def zero():
        return jnp.zeros((columns, size), F32)

    def ratio(top, bottom):
        return jnp.where(bottom > 0.0, top / jnp.where(bottom > 0.0, bottom, 1.0), 0.0)

    def factor(t, last):
        i, j = source(t)
        w[t] = lanes([shared[i, pl.ds(tail + j * halves + k, 1), :] for k in range(halves)])
        rate = shared[i, pl.ds(tail + per_segment * halves + j, 1), :]
        link = rate * last
        inverse_pivot = 1.0 / (1.0 + rate * rate - rate * link)
        rates[t] = lanes([rate] * halves)
        e[t] = lanes([link] * halves)
        d[t] = lanes([inverse_pivot] * halves)
        return inverse_pivot

    loop(steps, factor, jnp.zeros((1, LANES), F32))

    biggest = loop(steps, lambda t, acc: jnp.maximum(acc, jnp.abs(right_side(t))), zero())
    biggest = jnp.max(biggest, axis=1, keepdims=True)
    biggest = jnp.where(biggest > 0.0, biggest, 1.0)
    shrink = 1.0 / biggest

    def load(t, carry):
        r[at(t), :] = right_side(t) * shrink
        return carry

    loop(steps, load, 0)

    def down(t, last):
        value = z[at(t), :] + e[t] * last
        z[at(t), :] = value
        return value

    def start(first):
        z[...] = exact_dot(r[...], g[...])
        loop(steps, down, zero())

        def up(k, carry):
            above, acc = carry
            t = steps - 1 - k
            value = z[at(t), :] * d[t] + above
            x[at(t), :] = value if first else x[at(t), :] + value
            r[at(t), :] = value
            p[at(t), :] = value
            return e[t] * value, acc + w[t] * value * value

        unused, acc = loop(steps, up, (zero(), zero()))
        return over_lanes(acc)

    def weigh(t, carry):
        z[at(t), :] = w[t] * p[at(t), :]
        return carry

    def step(state):
        count, square, limit, unused = state
        loop(steps, weigh, 0)
        z[...] = split_dot(z[...], g_high[...], g_low[...])
        loop(steps, down, zero())

        def up(k, carry):
            above, own, cross = carry
            t = steps - 1 - k
            value = z[at(t), :] * d[t] + above
            z[at(t), :] = value
            direction = p[at(t), :]
            weighted = w[t] * direction
            return e[t] * value, own + weighted * direction, cross + weighted * value

        unused, own, cross = loop(steps, up, (zero(), zero(), zero()))
        own, cross = over_lanes(own), over_lanes(cross)
        alpha = ratio(square, own + cross)

        def advance(t, acc):
            change = z[at(t), :]
            x[at(t), :] -= alpha * change
            value = r[at(t), :] - alpha * (p[at(t), :] + change)
            r[at(t), :] = value
            return acc + w[t] * value * value

        new_square = over_lanes(loop(steps, advance, zero()))
        beta = ratio(new_square, square)

        def turn(t, carry):
            p[at(t), :] = r[at(t), :] + beta * p[at(t), :]
            return carry

        loop(steps, turn, 0)
        share = ratio(cross, own + cross)
        return count + 1, new_square, limit, jnp.max(share * share * new_square - limit)

    def goes_on(state):
        count, unused, unused_limit, excess = state
        return jnp.logical_and(count < STEP_LIMIT, excess > 0.0)

    def iterate(square):
        return lax.while_loop(goes_on, step, (0, square, square * TOLERANCE**2, jnp.max(square)))[0]

    whole_square = start(True)
    count = iterate(whole_square)

    def refine(state):
        count, unused = state

        def combine(t, last):
            here = x[at(t), :]
            after = jnp.minimum(t + 1, steps - 1)
            link = jnp.where(t + 1 < steps, 1.0, 0.0) * rates[after]
            value = (1.0 + rates[t] * rates[t]) * here - rates[t] * last - link * x[at(after), :]
            z[at(t), :] = value
            return here

        lax.fori_loop(0, steps, combine, zero())
        z[...] = exact_dot(z[...], spatial[...])

        def subtract(t, carry):
            i, j = source(t)
            r[at(t), :] = right_side(t) * shrink - z[at(t), :] - w[t] * x[at(t), :]
            return carry

        lax.fori_loop(0, steps, subtract, 0)
        square = start(False)
        iterate(square)
        return count + 1, jnp.max(square - whole_square * CORRECTION_TOLERANCE**2)

    def refines(state):
        count, excess = state
        return jnp.logical_and(count < REFINEMENT_LIMIT, excess > 0.0)

    needed = jnp.logical_or(error[0, 0] > INVERSE_TOLERANCE**2, count > EASY_STEPS)
    lax.while_loop(refines, refine, (0, jnp.where(needed, 1.0, 0.0)))

    def store(t, carry):
        i, j = source(t)
        out[i, rows(j * columns), :] = x[at(t), :] * biggest
        return carry

    loop(steps, store, 0)


def solve(received, shared, spatial, inverse, segments, per_segment, columns):
    size = spatial.shape[0]
    steps = segments * per_segment
    state = pltpu.VMEM((steps * columns, size), F32)
    per_step = pltpu.VMEM((steps, 1, size), F32)
    full, high, low, error = inverse
    vmem, smem = pl.BlockSpec(memory_space=pltpu.VMEM), pl.BlockSpec(memory_space=pltpu.SMEM)
    return pl.pallas_call(
        functools.partial(solve_kernel, segments, per_segment, columns),
        out_shape=jax.ShapeDtypeStruct((segments, per_segment * columns, size), F32),
        in_specs=[vmem, vmem, smem, vmem, vmem, vmem, vmem],
        out_specs=vmem,
        scratch_shapes=[state] * 4 + [per_step] * 4,
        compiler_params=pltpu.CompilerParams(vmem_limit_bytes=40 * 2**20),
        name="solve",
    )(received, shared, error, spatial, full, high, low)


def pad_columns(received, per_segment, halves, columns, padded):
    devices, total, width = received.shape
    rows = per_segment * halves * columns
    block = received[:, :rows].reshape(devices, per_segment * halves, columns, width)
    block = jnp.pad(block, ((0, 0), (0, 0), (0, padded - columns), (0, 0)))
    return jnp.concatenate([block.reshape(devices, -1, width), received[:, rows:]], axis=1)


def body(spatial, persistence, obs_weight, right_side):
    devices = lax.axis_size("tm")
    per_segment, size, column_count = right_side.shape
    halves = size // LANES
    chunks = CHUNKS if column_count // devices % (CHUNKS * SUBLANES) == 0 else 1
    columns = column_count // devices // chunks
    padded = -(-columns // SUBLANES) * SUBLANES
    inverse = invert_spatial(spatial)
    packed = pack(persistence, right_side, obs_weight, devices, chunks)
    received = [lax.all_to_all(chunk, "tm", 0, 0, tiled=True) for chunk in packed]
    returned = []
    for chunk in received:
        if padded != columns:
            chunk = pad_columns(chunk, per_segment, halves, columns, padded)
        solved = solve(chunk, received[0], spatial, inverse, devices, per_segment, padded)
        if padded != columns:
            solved = solved.reshape(devices, per_segment, padded, size)[:, :, :columns]
            solved = solved.reshape(devices, per_segment * columns, size)
        solved = lax.all_to_all(solved, "tm", 0, 0, tiled=True)
        returned.append(solved.reshape(devices, per_segment, columns, size))
    returned = jnp.stack(returned, axis=2)
    return jnp.transpose(returned, (1, 4, 0, 2, 3)).reshape(per_segment, size, column_count)


def solution(mesh):
    placed = (P(), P(("groups", "tm")), P(("groups", "tm"), None), P(("groups", "tm"), None, None))
    return jax.shard_map(
        body, mesh=mesh, in_specs=placed, out_specs=P(("groups", "tm"), None, None), check_vma=False
    )
```

```python
import functools

import jax
import jax.numpy as jnp
from jax import lax
from jax.experimental import pallas as pl
from jax.experimental.pallas import tpu as pltpu
from jax.sharding import PartitionSpec as P

F32 = jnp.float32
BF16 = jnp.bfloat16
SUBLANES = 8
LANES = 128
MATRIX_ROWS = 512
WRITTEN_OUT = 1
UNCHECKED_STEPS = 2
TOLERANCE = 1e-5
STEP_LIMIT = 2000
COARSE_LIMIT = 14
FINE_LIMIT = 80
INVERSE_TOLERANCE = 1e-5
EASY_STEPS = 6
CORRECTION_TOLERANCE = 1e-6
REFINEMENT_LIMIT = 8


def split(value):
    high = value.astype(BF16)
    return high, (value - high.astype(F32)).astype(BF16)


def dot(left, right):
    return jnp.dot(left, right, preferred_element_type=F32)


def split_dot(left, right_high, right_low):
    high, low = split(left)
    return dot(high, right_high) + dot(low, right_high) + dot(high, right_low)


def exact_dot(left, right):
    return jnp.dot(left, right, preferred_element_type=F32, precision=lax.Precision.HIGHEST)


def loop(count, body, start):
    if count <= WRITTEN_OUT:
        carry = start
        for i in range(count):
            carry = body(i, carry)
        return carry
    return lax.fori_loop(0, count, body, start)


def eye(size):
    rows = lax.broadcasted_iota(jnp.int32, (size, size), 0)
    columns = lax.broadcasted_iota(jnp.int32, (size, size), 1)
    return jnp.where(rows == columns, 1.0, 0.0).astype(F32)


def row_sum_norm(value):
    return jnp.max(jnp.sum(jnp.abs(value), axis=0, keepdims=True))


def invert(spatial, inverse):
    size = spatial.shape[0]
    identity = eye(size)
    high = spatial.astype(BF16)
    square = dot(high, high)
    bound = jnp.sqrt(row_sum_norm(square)) * 1.02
    scale = 1.9 / bound
    start = scale * (2.0 * identity - scale * spatial)
    inverse[...] = start

    def coarse_step(state):
        count, unused = state
        guess = inverse[...]
        residual = identity - dot(high, guess.astype(BF16))
        inverse[...] = guess + dot(guess.astype(BF16), residual.astype(BF16))
        return count + 1, row_sum_norm(residual)

    def coarse_goes_on(state):
        count, error = state
        return jnp.logical_and(count < COARSE_LIMIT, error > 0.3)

    unused, error = lax.while_loop(coarse_goes_on, coarse_step, (0, F32(1e30)))

    @pl.when(jnp.logical_not(error <= 0.3))
    def restart():
        inverse[...] = start

    def fine_step(state):
        count, unused = state
        guess = inverse[...]
        residual = identity - exact_dot(spatial, guess)
        inverse[...] = guess + exact_dot(guess, residual)
        return count + 1, row_sum_norm(residual)

    def fine_goes_on(state):
        count, error = state
        return jnp.logical_and(count < FINE_LIMIT, error > 1e-3)

    lax.while_loop(fine_goes_on, fine_step, (0, F32(1e30)))
    result = inverse[...]
    result = 0.5 * (result + result.T)
    inverse[...] = result
    residual = identity - exact_dot(spatial, result)
    return jnp.sum(residual * residual) / size


def invert_kernel(spatial, inverse, high, low, error):
    error[0, 0] = invert(spatial[...], inverse)
    high[...], low[...] = split(inverse[...])


def invert_spatial(spatial):
    size = spatial.shape[0]
    half = jax.ShapeDtypeStruct((size, size), BF16)
    full = jax.ShapeDtypeStruct((size, size), F32)
    vmem, smem = pl.BlockSpec(memory_space=pltpu.VMEM), pl.BlockSpec(memory_space=pltpu.SMEM)
    return pl.pallas_call(
        invert_kernel,
        out_shape=[full, half, half, jax.ShapeDtypeStruct((1, 1), F32)],
        in_specs=[vmem],
        out_specs=[vmem, vmem, vmem, smem],
        cost_estimate=pl.CostEstimate(flops=80 * size**3, bytes_accessed=16 * size**2, transcendentals=0),
        compiler_params=pltpu.CompilerParams(vmem_limit_bytes=16 * 2**20),
        name="invert",
    )(spatial)


def tail_rows(per_segment, halves):
    rows = per_segment * halves + per_segment
    return rows + -rows % SUBLANES


def pack_kernel(rates, right_side, weights, out, turned, source, rate, weight, arrivals, departures):
    steps, size, column_count = right_side.shape
    devices = out.shape[0]
    columns = column_count // devices
    halves = size // LANES
    rows = halves * columns
    tail = tail_rows(steps, halves)
    loads = [pltpu.make_async_copy(right_side.at[e], source.at[e], arrivals.at[e]) for e in range(steps)]
    loads.append(pltpu.make_async_copy(rates, rate, arrivals.at[steps]))
    loads.append(pltpu.make_async_copy(weights, weight, arrivals.at[steps + 1]))
    for copy in loads:
        copy.start()
    sizes = [rows] * (steps - 1) + [rows + tail]
    stores = []
    for e in range(steps):
        part = pl.ds(e * rows, sizes[e])
        stores.append(pltpu.make_async_copy(turned.at[:, part, :], out.at[:, part, :], departures.at[e]))
    for e in range(steps):
        loads[e].wait()
        value = source[e].T
        for i in range(devices):
            for k in range(halves):
                turned[i, pl.ds(e * rows + k * columns, columns), :] = value[
                    i * columns : (i + 1) * columns, k * LANES : (k + 1) * LANES
                ]
        if e == steps - 1:
            for copy in loads[steps:]:
                copy.wait()
            row = lax.broadcasted_iota(jnp.int32, (tail, LANES), 0)
            last = jnp.zeros(row.shape, F32)
            for j in range(steps):
                for k in range(halves):
                    piece = weight[pl.ds(j, 1), pl.ds(k * LANES, LANES)]
                    last = jnp.where(row == j * halves + k, piece, last)
                last = jnp.where(row == steps * halves + j, rate[j], last)
            for i in range(devices):
                turned[i, pl.ds(steps * rows, tail), :] = last
        stores[e].start()
    for copy in stores:
        copy.wait()


def pack(persistence, right_side, weights, devices):
    steps, size, column_count = right_side.shape
    halves = size // LANES
    total = steps * halves * (column_count // devices) + tail_rows(steps, halves)
    anywhere = pl.BlockSpec(memory_space=pl.ANY)
    shape = (devices, total, LANES)
    return pl.pallas_call(
        pack_kernel,
        out_shape=jax.ShapeDtypeStruct(shape, F32),
        in_specs=[anywhere] * 3,
        out_specs=anywhere,
        scratch_shapes=[
            pltpu.VMEM(shape, F32),
            pltpu.VMEM(right_side.shape, F32),
            pltpu.SMEM(persistence.shape, F32),
            pltpu.VMEM(weights.shape, F32),
            pltpu.SemaphoreType.DMA((steps + 2,)),
            pltpu.SemaphoreType.DMA((steps,)),
        ],
        compiler_params=pltpu.CompilerParams(vmem_limit_bytes=56 * 2**20),
        name="pack",
    )(persistence, right_side, weights)


def solve_kernel(
    segments, per_segment, columns,
    received, error, spatial, g, g_high, g_low, out,
    x, r, p, z, w, e, d, rates,
):
    size = g.shape[0]
    steps = segments * per_segment
    halves = size // LANES
    tail = received.shape[1] - tail_rows(per_segment, halves)
    group = max(MATRIX_ROWS // columns, 1)
    if steps % group:
        group = 1
    groups = steps // group

    def rows(start):
        if isinstance(start, int):
            return pl.ds(start, columns)
        return pl.ds(pl.multiple_of(start, SUBLANES), columns)

    def at(t):
        return rows(t * columns)

    def source(t):
        if isinstance(t, int):
            return t // per_segment, t % per_segment
        return lax.div(t, per_segment), lax.rem(t, per_segment)

    def lanes(pieces):
        return jnp.concatenate(pieces, axis=1)

    def right_side(t):
        i, j = source(t)
        return lanes([received[i, rows((j * halves + k) * columns), :] for k in range(halves)])

    def at_step(ref, t):
        return lanes([ref[pl.ds(t, 1), :]] * halves)

    def over_lanes(value):
        return jnp.sum(value, axis=1, keepdims=True)

    def zero():
        return jnp.zeros((columns, size), F32)

    def ratio(top, bottom):
        return jnp.where(bottom > 0.0, top / jnp.where(bottom > 0.0, bottom, 1.0), 0.0)

    def over_steps(body, start):
        def over_group(i, carry):
            for k in range(group):
                carry = body(i * group + k, carry)
            return carry

        return loop(groups, over_group, start)

    def over_steps_back(body, start):
        def over_group(i, carry):
            for k in reversed(range(group)):
                carry = body((groups - 1 - i) * group + k, carry)
            return carry

        return loop(groups, over_group, start)

    def gather(t, carry):
        i, j = source(t)
        w[t] = lanes([received[i, pl.ds(tail + j * halves + k, 1), :] for k in range(halves)])
        rates[pl.ds(t, 1), :] = received[i, pl.ds(tail + per_segment * halves + j, 1), :]
        return carry

    over_steps(gather, 0)
    e[...] = 1.0 / (rates[...] * rates[...])

    def pivot(t, last):
        value = e[pl.ds(t, 1), :] * (last + 1.0)
        d[pl.ds(t, 1), :] = value
        return value

    over_steps(pivot, jnp.zeros((1, LANES), F32))
    pivots = d[...] / (d[...] + 1.0)
    d[...] = pivots
    first_step = lax.broadcasted_iota(jnp.int32, pivots.shape, 0) == 0
    e[...] = rates[...] * jnp.where(first_step, 0.0, pltpu.roll(pivots, 1, 0))

    biggest = over_steps(lambda t, acc: jnp.maximum(acc, jnp.abs(right_side(t))), zero())
    biggest = jnp.max(biggest, axis=1, keepdims=True)
    biggest = jnp.where(biggest > 0.0, biggest, 1.0)
    shrink = 1.0 / biggest

    def start(first):
        def down(i, last):
            ts = [i * group + k for k in range(group)]
            value = jnp.concatenate([right_side(t) if first else r[at(t), :] for t in ts], axis=0)
            value = exact_dot(value, g[...])
            for k, t in enumerate(ts):
                piece = value[k * columns : (k + 1) * columns]
                if first:
                    piece = piece * shrink
                last = piece + at_step(e, t) * last
                z[at(t), :] = last
            return last

        loop(groups, down, zero())

        def up(t, carry):
            above, acc = carry
            value = z[at(t), :] * at_step(d, t) + above
            x[at(t), :] = value if first else x[at(t), :] + value
            r[at(t), :] = value
            p[at(t), :] = value
            return at_step(e, t) * value, acc + w[t] * value * value

        unused, acc = over_steps_back(up, (zero(), zero()))
        return over_lanes(acc)

    def step(state):
        square, beta = state

        def down(i, last):
            ts = [i * group + k for k in range(group)]
            pieces = []
            for t in ts:
                direction = r[at(t), :] + beta * p[at(t), :]
                p[at(t), :] = direction
                pieces.append(w[t] * direction)
            value = split_dot(jnp.concatenate(pieces, axis=0), g_high[...], g_low[...])
            for k, t in enumerate(ts):
                last = value[k * columns : (k + 1) * columns] + at_step(e, t) * last
                z[at(t), :] = last
            return last

        loop(groups, down, zero())

        def up(t, carry):
            above, own, cross = carry
            value = z[at(t), :] * at_step(d, t) + above
            z[at(t), :] = value
            direction = p[at(t), :]
            weighted = w[t] * direction
            return at_step(e, t) * value, own + weighted * direction, cross + weighted * value

        unused, own, cross = over_steps_back(up, (zero(), zero(), zero()))
        own, cross = over_lanes(own), over_lanes(cross)
        alpha = ratio(square, own + cross)

        def advance(t, acc):
            change = z[at(t), :]
            x[at(t), :] -= alpha * change
            value = r[at(t), :] - alpha * (p[at(t), :] + change)
            r[at(t), :] = value
            return acc + w[t] * value * value

        new_square = over_lanes(over_steps(advance, zero()))
        share = ratio(cross, own + cross)
        return new_square, ratio(new_square, square), share * share * new_square

    def iterate(square):
        limit = square * TOLERANCE**2
        state = lax.fori_loop(
            0, UNCHECKED_STEPS, lambda i, state: step(state)[:2], (square, jnp.zeros_like(square))
        )

        def goes_on(state):
            count, unused, unused_beta, excess = state
            return jnp.logical_and(count < STEP_LIMIT, excess > 0.0)

        def checked(state):
            count, square, beta, unused = state
            square, beta, left = step((square, beta))
            return count + 1, square, beta, jnp.max(left - limit)

        return lax.while_loop(goes_on, checked, (UNCHECKED_STEPS, *state, F32(1.0)))[0]

    whole_square = start(True)
    count = iterate(whole_square)

    def refine(state):
        count, unused = state

        def combine(t, last):
            here = x[at(t), :]
            after = jnp.minimum(t + 1, steps - 1)
            link = jnp.where(t + 1 < steps, 1.0, 0.0) * at_step(rates, after)
            rate = at_step(rates, t)
            z[at(t), :] = (1.0 + rate * rate) * here - rate * last - link * x[at(after), :]
            return here

        lax.fori_loop(0, steps, combine, zero())
        z[...] = exact_dot(z[...], spatial[...])

        def subtract(t, carry):
            r[at(t), :] = right_side(t) * shrink - z[at(t), :] - w[t] * x[at(t), :]
            return carry

        lax.fori_loop(0, steps, subtract, 0)
        square = start(False)
        iterate(square)
        return count + 1, jnp.max(square - whole_square * CORRECTION_TOLERANCE**2)

    def refines(state):
        count, excess = state
        return jnp.logical_and(count < REFINEMENT_LIMIT, excess > 0.0)

    needed = jnp.logical_or(error[0, 0] > INVERSE_TOLERANCE**2, count > EASY_STEPS)
    lax.while_loop(refines, refine, (0, jnp.where(needed, 1.0, 0.0)))

    def store(t, carry):
        i, j = source(t)
        out[i, rows(j * columns), :] = x[at(t), :] * biggest
        return carry

    over_steps(store, 0)


def solve(received, spatial, inverse, segments, per_segment, columns):
    size = spatial.shape[0]
    steps = segments * per_segment
    state = pltpu.VMEM((steps * columns, size), F32)
    per_step = pltpu.VMEM((steps, LANES), F32)
    full, high, low, error = inverse
    vmem, smem = pl.BlockSpec(memory_space=pltpu.VMEM), pl.BlockSpec(memory_space=pltpu.SMEM)
    return pl.pallas_call(
        functools.partial(solve_kernel, segments, per_segment, columns),
        out_shape=jax.ShapeDtypeStruct((segments, per_segment * columns, size), F32),
        in_specs=[vmem, smem, vmem, vmem, vmem, vmem],
        out_specs=vmem,
        scratch_shapes=[state] * 4 + [pltpu.VMEM((steps, 1, size), F32)] + [per_step] * 3,
        compiler_params=pltpu.CompilerParams(vmem_limit_bytes=40 * 2**20),
        name="solve",
    )(received, error, spatial, full, high, low)


def pad_columns(received, per_segment, halves, columns, padded):
    devices, total, width = received.shape
    rows = per_segment * halves * columns
    block = received[:, :rows].reshape(devices, per_segment * halves, columns, width)
    block = jnp.pad(block, ((0, 0), (0, 0), (0, padded - columns), (0, 0)))
    return jnp.concatenate([block.reshape(devices, -1, width), received[:, rows:]], axis=1)


def body(spatial, persistence, obs_weight, right_side):
    devices = lax.axis_size("tm")
    per_segment, size, column_count = right_side.shape
    columns = column_count // devices
    padded = -(-columns // SUBLANES) * SUBLANES
    inverse = invert_spatial(spatial)
    packed = pack(persistence, right_side, obs_weight, devices)
    received = lax.all_to_all(packed, "tm", 0, 0, tiled=True)
    if padded != columns:
        received = pad_columns(received, per_segment, size // LANES, columns, padded)
    solved = solve(received, spatial, inverse, devices, per_segment, padded)
    if padded != columns:
        solved = solved.reshape(devices, per_segment, padded, size)[:, :, :columns]
        solved = solved.reshape(devices, per_segment * columns, size)
    returned = lax.all_to_all(solved, "tm", 0, 0, tiled=True)
    returned = returned.reshape(devices, per_segment, columns, size)
    return jnp.transpose(returned, (1, 3, 0, 2)).reshape(per_segment, size, column_count)


def solution(mesh):
    placed = (P(), P(("groups", "tm")), P(("groups", "tm"), None), P(("groups", "tm"), None, None))
    return jax.shard_map(
        body, mesh=mesh, in_specs=placed, out_specs=P(("groups", "tm"), None, None), check_vma=False
    )
```

```python
import functools

import jax
import jax.numpy as jnp
from jax import lax
from jax.experimental import pallas as pl
from jax.experimental.pallas import tpu as pltpu
from jax.sharding import PartitionSpec as P

F32 = jnp.float32
BF16 = jnp.bfloat16
SUBLANES = 8
LANES = 128
MATRIX_ROWS = 512
WRITTEN_OUT = 1
UNCHECKED_STEPS = 2
TOLERANCE = 1e-5
STEP_LIMIT = 2000
COARSE_LIMIT = 14
FINE_LIMIT = 80
INVERSE_TOLERANCE = 1e-5
EASY_STEPS = 6
CORRECTION_TOLERANCE = 1e-6
REFINEMENT_LIMIT = 8


def split(value):
    high = value.astype(BF16)
    return high, (value - high.astype(F32)).astype(BF16)


def dot(left, right):
    return jnp.dot(left, right, preferred_element_type=F32)


def split_dot(left, right_high, right_low):
    high, low = split(left)
    return dot(high, right_high) + dot(low, right_high) + dot(high, right_low)


def exact_dot(left, right):
    return jnp.dot(left, right, preferred_element_type=F32, precision=lax.Precision.HIGHEST)


def loop(count, body, start):
    if count <= WRITTEN_OUT:
        carry = start
        for i in range(count):
            carry = body(i, carry)
        return carry
    return lax.fori_loop(0, count, body, start)


def eye(size):
    rows = lax.broadcasted_iota(jnp.int32, (size, size), 0)
    columns = lax.broadcasted_iota(jnp.int32, (size, size), 1)
    return jnp.where(rows == columns, 1.0, 0.0).astype(F32)


def row_sum_norm(value):
    return jnp.max(jnp.sum(jnp.abs(value), axis=0, keepdims=True))


def invert(spatial, inverse):
    size = spatial.shape[0]
    identity = eye(size)
    high = spatial.astype(BF16)
    square = dot(high, high)
    bound = jnp.sqrt(row_sum_norm(square)) * 1.02
    scale = 1.9 / bound
    start = scale * (2.0 * identity - scale * spatial)
    inverse[...] = start

    def coarse_step(state):
        count, unused = state
        guess = inverse[...]
        residual = identity - dot(high, guess.astype(BF16))
        inverse[...] = guess + dot(guess.astype(BF16), residual.astype(BF16))
        return count + 1, row_sum_norm(residual)

    def coarse_goes_on(state):
        count, error = state
        return jnp.logical_and(count < COARSE_LIMIT, error > 0.3)

    unused, error = lax.while_loop(coarse_goes_on, coarse_step, (0, F32(1e30)))

    @pl.when(jnp.logical_not(error <= 0.3))
    def restart():
        inverse[...] = start

    def fine_step(state):
        count, unused = state
        guess = inverse[...]
        residual = identity - exact_dot(spatial, guess)
        inverse[...] = guess + exact_dot(guess, residual)
        return count + 1, row_sum_norm(residual)

    def fine_goes_on(state):
        count, error = state
        return jnp.logical_and(count < FINE_LIMIT, error > 1e-3)

    lax.while_loop(fine_goes_on, fine_step, (0, F32(1e30)))
    result = inverse[...]
    result = 0.5 * (result + result.T)
    inverse[...] = result
    residual = identity - exact_dot(spatial, result)
    return jnp.sum(residual * residual) / size


def invert_kernel(spatial, inverse, high, low, error):
    error[0, 0] = invert(spatial[...], inverse)
    high[...], low[...] = split(inverse[...])


def invert_spatial(spatial):
    size = spatial.shape[0]
    half = jax.ShapeDtypeStruct((size, size), BF16)
    full = jax.ShapeDtypeStruct((size, size), F32)
    vmem, smem = pl.BlockSpec(memory_space=pltpu.VMEM), pl.BlockSpec(memory_space=pltpu.SMEM)
    return pl.pallas_call(
        invert_kernel,
        out_shape=[full, half, half, jax.ShapeDtypeStruct((1, 1), F32)],
        in_specs=[vmem],
        out_specs=[vmem, vmem, vmem, smem],
        cost_estimate=pl.CostEstimate(flops=80 * size**3, bytes_accessed=16 * size**2, transcendentals=0),
        compiler_params=pltpu.CompilerParams(vmem_limit_bytes=16 * 2**20),
        name="invert",
    )(spatial)


def tail_rows(per_segment, halves):
    rows = per_segment * halves + per_segment
    return rows + -rows % SUBLANES


def pack_kernel(rates, right_side, weights, out, turned, source, rate, weight, arrivals, departures):
    steps, size, column_count = right_side.shape
    devices = out.shape[0]
    columns = column_count // devices
    halves = size // LANES
    rows = halves * columns
    tail = tail_rows(steps, halves)
    loads = [pltpu.make_async_copy(right_side.at[e], source.at[e], arrivals.at[e]) for e in range(steps)]
    loads.append(pltpu.make_async_copy(rates, rate, arrivals.at[steps]))
    loads.append(pltpu.make_async_copy(weights, weight, arrivals.at[steps + 1]))
    for copy in loads:
        copy.start()
    sizes = [rows] * (steps - 1) + [rows + tail]
    stores = []
    for e in range(steps):
        part = pl.ds(e * rows, sizes[e])
        stores.append(pltpu.make_async_copy(turned.at[:, part, :], out.at[:, part, :], departures.at[e]))
    for e in range(steps):
        loads[e].wait()
        value = source[e].T
        for i in range(devices):
            for k in range(halves):
                turned[i, pl.ds(e * rows + k * columns, columns), :] = value[
                    i * columns : (i + 1) * columns, k * LANES : (k + 1) * LANES
                ]
        if e == steps - 1:
            for copy in loads[steps:]:
                copy.wait()
            row = lax.broadcasted_iota(jnp.int32, (tail, LANES), 0)
            last = jnp.zeros(row.shape, F32)
            for j in range(steps):
                for k in range(halves):
                    piece = weight[pl.ds(j, 1), pl.ds(k * LANES, LANES)]
                    last = jnp.where(row == j * halves + k, piece, last)
                last = jnp.where(row == steps * halves + j, rate[j], last)
            for i in range(devices):
                turned[i, pl.ds(steps * rows, tail), :] = last
        stores[e].start()
    for copy in stores:
        copy.wait()


def pack(persistence, right_side, weights, devices):
    steps, size, column_count = right_side.shape
    halves = size // LANES
    total = steps * halves * (column_count // devices) + tail_rows(steps, halves)
    anywhere = pl.BlockSpec(memory_space=pl.ANY)
    shape = (devices, total, LANES)
    return pl.pallas_call(
        pack_kernel,
        out_shape=jax.ShapeDtypeStruct(shape, F32),
        in_specs=[anywhere] * 3,
        out_specs=anywhere,
        scratch_shapes=[
            pltpu.VMEM(shape, F32),
            pltpu.VMEM(right_side.shape, F32),
            pltpu.SMEM(persistence.shape, F32),
            pltpu.VMEM(weights.shape, F32),
            pltpu.SemaphoreType.DMA((steps + 2,)),
            pltpu.SemaphoreType.DMA((steps,)),
        ],
        compiler_params=pltpu.CompilerParams(vmem_limit_bytes=56 * 2**20),
        name="pack",
    )(persistence, right_side, weights)


def solve_kernel(
    segments, per_segment, columns,
    received, error, spatial, g, g_high, g_low, out,
    x, r, p, z, w, e, d, rates,
):
    size = g.shape[0]
    steps = segments * per_segment
    halves = size // LANES
    tail = received.shape[1] - tail_rows(per_segment, halves)
    group = max(MATRIX_ROWS // columns, 1)
    if steps % group:
        group = 1
    groups = steps // group

    def rows(start):
        if isinstance(start, int):
            return pl.ds(start, columns)
        return pl.ds(pl.multiple_of(start, SUBLANES), columns)

    def at(t):
        return rows(t * columns)

    def source(t):
        if isinstance(t, int):
            return t // per_segment, t % per_segment
        return lax.div(t, per_segment), lax.rem(t, per_segment)

    def lanes(pieces):
        return jnp.concatenate(pieces, axis=1)

    def right_side(t):
        i, j = source(t)
        return lanes([received[i, rows((j * halves + k) * columns), :] for k in range(halves)])

    def at_step(ref, t):
        return lanes([ref[pl.ds(t, 1), :]] * halves)

    def over_lanes(value):
        return jnp.sum(value, axis=1, keepdims=True)

    def zero():
        return jnp.zeros((columns, size), F32)

    def ratio(top, bottom):
        return jnp.where(bottom > 0.0, top / jnp.where(bottom > 0.0, bottom, 1.0), 0.0)

    def over_steps(body, start):
        def over_group(i, carry):
            for k in range(group):
                carry = body(i * group + k, carry)
            return carry

        return loop(groups, over_group, start)

    def over_steps_back(body, start):
        def over_group(i, carry):
            for k in reversed(range(group)):
                carry = body((groups - 1 - i) * group + k, carry)
            return carry

        return loop(groups, over_group, start)

    def gather(t, carry):
        i, j = source(t)
        w[t] = lanes([received[i, pl.ds(tail + j * halves + k, 1), :] for k in range(halves)])
        rates[pl.ds(t, 1), :] = received[i, pl.ds(tail + per_segment * halves + j, 1), :]
        return carry

    over_steps(gather, 0)
    e[...] = 1.0 / (rates[...] * rates[...])

    def pivot(t, last):
        value = e[pl.ds(t, 1), :] * (last + 1.0)
        d[pl.ds(t, 1), :] = value
        return value

    over_steps(pivot, jnp.zeros((1, LANES), F32))
    pivots = d[...] / (d[...] + 1.0)
    d[...] = pivots
    first_step = lax.broadcasted_iota(jnp.int32, pivots.shape, 0) == 0
    e[...] = rates[...] * jnp.where(first_step, 0.0, pltpu.roll(pivots, 1, 0))

    biggest = over_steps(lambda t, acc: jnp.maximum(acc, jnp.abs(right_side(t))), zero())
    biggest = jnp.max(biggest, axis=1, keepdims=True)
    biggest = jnp.where(biggest > 0.0, biggest, 1.0)
    shrink = 1.0 / biggest

    def start(first):
        def down(i, last):
            ts = [i * group + k for k in range(group)]
            value = jnp.concatenate([right_side(t) if first else r[at(t), :] for t in ts], axis=0)
            value = exact_dot(value, g[...])
            for k, t in enumerate(ts):
                piece = value[k * columns : (k + 1) * columns]
                if first:
                    piece = piece * shrink
                last = piece + at_step(e, t) * last
                z[at(t), :] = last
            return last

        loop(groups, down, zero())

        def up(t, carry):
            above, acc = carry
            value = z[at(t), :] * at_step(d, t) + above
            x[at(t), :] = value if first else x[at(t), :] + value
            r[at(t), :] = value
            p[at(t), :] = value
            return at_step(e, t) * value, acc + w[t] * value * value

        unused, acc = over_steps_back(up, (zero(), zero()))
        return over_lanes(acc)

    def turn(square, beta):
        def down(i, last):
            ts = [i * group + k for k in range(group)]
            pieces = []
            for t in ts:
                direction = r[at(t), :] + beta * p[at(t), :]
                p[at(t), :] = direction
                pieces.append(w[t] * direction)
            value = split_dot(jnp.concatenate(pieces, axis=0), g_high[...], g_low[...])
            for k, t in enumerate(ts):
                last = value[k * columns : (k + 1) * columns] + at_step(e, t) * last
                z[at(t), :] = last
            return last

        loop(groups, down, zero())

        def up(t, carry):
            above, own, cross, image = carry
            value = z[at(t), :] * at_step(d, t) + above
            z[at(t), :] = value
            direction = p[at(t), :]
            weighted = w[t] * direction
            both = w[t] * value
            own, cross, image = own + weighted * direction, cross + weighted * value, image + both * value
            return at_step(e, t) * value, own, cross, image

        unused, own, cross, image = over_steps_back(up, (zero(), zero(), zero(), zero()))
        own, cross, image = over_lanes(own), over_lanes(cross), over_lanes(image)
        alpha = ratio(square, own + cross)
        after = jnp.maximum(alpha * alpha * (own + 2.0 * cross + image) - square, 0.0)
        share = ratio(cross, own + cross)
        return alpha, share * share * after

    def advance(square, alpha):
        def move(t, acc):
            change = z[at(t), :]
            x[at(t), :] -= alpha * change
            value = r[at(t), :] - alpha * (p[at(t), :] + change)
            r[at(t), :] = value
            return acc + w[t] * value * value

        new_square = over_lanes(over_steps(move, zero()))
        return new_square, ratio(new_square, square)

    def iterate(square):
        limit = square * TOLERANCE**2

        def unchecked(i, state):
            square, beta = state
            return advance(square, turn(square, beta)[0])

        square, beta = lax.fori_loop(0, UNCHECKED_STEPS, unchecked, (square, jnp.zeros_like(square)))

        def goes_on(state):
            count, unused, unused_beta, unused_alpha, excess = state
            return jnp.logical_and(count < STEP_LIMIT, excess > 0.0)

        def checked(state):
            count, square, beta, alpha, unused = state
            alpha, left = turn(square, beta)
            excess = jnp.max(left - limit)

            def more():
                return advance(square, alpha)

            square, beta = lax.cond(excess > 0.0, more, lambda: (square, beta))
            return count + 1, square, beta, jnp.where(excess > 0.0, 0.0, alpha), excess

        state = (UNCHECKED_STEPS, square, beta, jnp.zeros_like(square), F32(1.0))
        state = lax.while_loop(goes_on, checked, state)
        return state[0], state[3]

    def finish(alpha):
        def move(t, carry):
            x[at(t), :] -= alpha * z[at(t), :]
            return carry

        lax.fori_loop(0, steps, move, 0)

    whole_square = start(True)
    count, alpha = iterate(whole_square)

    def refine(state):
        count, unused = state

        def combine(t, last):
            here = x[at(t), :]
            after = jnp.minimum(t + 1, steps - 1)
            link = jnp.where(t + 1 < steps, 1.0, 0.0) * at_step(rates, after)
            rate = at_step(rates, t)
            z[at(t), :] = (1.0 + rate * rate) * here - rate * last - link * x[at(after), :]
            return here

        lax.fori_loop(0, steps, combine, zero())
        z[...] = exact_dot(z[...], spatial[...])

        def subtract(t, carry):
            r[at(t), :] = right_side(t) * shrink - z[at(t), :] - w[t] * x[at(t), :]
            return carry

        lax.fori_loop(0, steps, subtract, 0)
        square = start(False)
        finish(iterate(square)[1])
        return count + 1, jnp.max(square - whole_square * CORRECTION_TOLERANCE**2)

    def refines(state):
        count, excess = state
        return jnp.logical_and(count < REFINEMENT_LIMIT, excess > 0.0)

    needed = jnp.logical_or(error[0, 0] > INVERSE_TOLERANCE**2, count > EASY_STEPS)

    def store(t, carry):
        i, j = source(t)
        out[i, rows(j * columns), :] = (x[at(t), :] - alpha * z[at(t), :]) * biggest
        return carry

    over_steps(store, 0)

    @pl.when(needed)
    def refined():
        finish(alpha)
        lax.while_loop(refines, refine, (0, F32(1.0)))

        def store_refined(t, carry):
            i, j = source(t)
            out[i, rows(j * columns), :] = x[at(t), :] * biggest
            return carry

        lax.fori_loop(0, steps, store_refined, 0)


def solve(received, spatial, inverse, segments, per_segment, columns):
    size = spatial.shape[0]
    steps = segments * per_segment
    state = pltpu.VMEM((steps * columns, size), F32)
    per_step = pltpu.VMEM((steps, LANES), F32)
    full, high, low, error = inverse
    vmem, smem = pl.BlockSpec(memory_space=pltpu.VMEM), pl.BlockSpec(memory_space=pltpu.SMEM)
    return pl.pallas_call(
        functools.partial(solve_kernel, segments, per_segment, columns),
        out_shape=jax.ShapeDtypeStruct((segments, per_segment * columns, size), F32),
        in_specs=[vmem, smem, vmem, vmem, vmem, vmem],
        out_specs=vmem,
        scratch_shapes=[state] * 4 + [pltpu.VMEM((steps, 1, size), F32)] + [per_step] * 3,
        compiler_params=pltpu.CompilerParams(vmem_limit_bytes=40 * 2**20),
        name="solve",
    )(received, error, spatial, full, high, low)


def unpack_kernel(returned, out, turned, departures):
    steps, size, column_count = out.shape
    devices = returned.shape[0]
    columns = column_count // devices
    spans = column_count // LANES
    per_span = devices // spans
    stores = []
    for e in range(steps):
        for k in range(spans):
            pieces = [returned[k * per_span + i, pl.ds(e * columns, columns), :] for i in range(per_span)]
            turned[e, k] = jnp.concatenate(pieces, axis=0).T
            some = out.at[e, :, pl.ds(k * LANES, LANES)]
            stores.append(pltpu.make_async_copy(turned.at[e, k], some, departures.at[e * spans + k]))
            stores[-1].start()
    for copy in stores:
        copy.wait()


def unpack(returned, steps, column_count):
    size = returned.shape[2]
    spans = column_count // LANES
    return pl.pallas_call(
        unpack_kernel,
        out_shape=jax.ShapeDtypeStruct((steps, size, column_count), F32),
        in_specs=[pl.BlockSpec(memory_space=pltpu.VMEM)],
        out_specs=pl.BlockSpec(memory_space=pl.ANY),
        scratch_shapes=[
            pltpu.VMEM((steps, spans, size, LANES), F32),
            pltpu.SemaphoreType.DMA((steps * spans,)),
        ],
        compiler_params=pltpu.CompilerParams(vmem_limit_bytes=16 * 2**20),
        name="unpack",
    )(returned)


def pad_columns(received, per_segment, halves, columns, padded):
    devices, total, width = received.shape
    rows = per_segment * halves * columns
    block = received[:, :rows].reshape(devices, per_segment * halves, columns, width)
    block = jnp.pad(block, ((0, 0), (0, 0), (0, padded - columns), (0, 0)))
    return jnp.concatenate([block.reshape(devices, -1, width), received[:, rows:]], axis=1)


def body(spatial, persistence, obs_weight, right_side):
    devices = lax.axis_size("tm")
    per_segment, size, column_count = right_side.shape
    columns = column_count // devices
    padded = -(-columns // SUBLANES) * SUBLANES
    inverse = invert_spatial(spatial)
    packed = pack(persistence, right_side, obs_weight, devices)
    received = lax.all_to_all(packed, "tm", 0, 0, tiled=True)
    if padded != columns:
        received = pad_columns(received, per_segment, size // LANES, columns, padded)
    solved = solve(received, spatial, inverse, devices, per_segment, padded)
    if padded != columns:
        solved = solved.reshape(devices, per_segment, padded, size)[:, :, :columns]
        solved = solved.reshape(devices, per_segment * columns, size)
    returned = lax.all_to_all(solved, "tm", 0, 0, tiled=True)
    if columns % SUBLANES == 0:
        return unpack(returned, per_segment, column_count)
    returned = returned.reshape(devices, per_segment, columns, size)
    return jnp.transpose(returned, (1, 3, 0, 2)).reshape(per_segment, size, column_count)


def solution(mesh):
    placed = (P(), P(("groups", "tm")), P(("groups", "tm"), None), P(("groups", "tm"), None, None))
    return jax.shard_map(
        body, mesh=mesh, in_specs=placed, out_specs=P(("groups", "tm"), None, None), check_vma=False
    )
```
